32 devices in a mesh: rep: 4 (over x, core), fsdp: 8 (over z, y).
Axes of the slice: x: 2, y: 2, z: 4, core: 2. Of those that a mesh axis runs over, the one named last changes fastest.
Arguments:
- replica_grads: bfloat16 [4, 8192, 8192], P('rep', 'fsdp'), may hold values from -0.19921875 to 0.19921875
- weight: bfloat16 [8192, 8192], P('fsdp'), may hold values from -6 to 6
- moment_one: float32 [1024, 1024], P('rep', 'fsdp'), may hold values from -3 to 3
- moment_two: float32 [1024, 1024], P('rep', 'fsdp'), may hold values from 0.1 to 10
- sign_bits: int32 [8192], replicated, may hold values from 0 to 1
- kept_rows: int32 [1024], replicated, may hold values from 0 to 8191, as said below
- step_count: int32 [], replicated, may hold values from 1 to 7
Outputs:
- new_weight: bfloat16 [8192, 8192], P('fsdp')
- new_moment_one: float32 [1024, 1024], P('rep', 'fsdp')
- new_moment_two: float32 [1024, 1024], P('rep', 'fsdp')
The draws below stay inside these ranges and needn't reach their ends.
Inputs may be any that keep to these rules, and one draw needn't show every extreme that they name: `kept_rows`: all different; 0 and 8191 are always among them.
All inputs are finite; a program needn't handle non-finite values.
Results may differ from the reference program's by a relative error of at most 0.0049.
Values may be sent and summed in bfloat16 or wider, within the bound.
A program may use at most 192 MiB of HBM per device.

```python
import math
import jax
import jax.numpy as jnp
from jax import lax

D = 8192
K = 1024
REPS = 4


def draw_kept_rows(key, part):
    first_key = jax.random.fold_in(key, 11)
    second_key = jax.random.fold_in(key, 23)
    others = jax.random.permutation(first_key, D - 2)[:K - 2].astype(jnp.int32) + 1
    values = jnp.concatenate([jnp.array([0, D - 1], jnp.int32), others])
    return jax.random.permutation(second_key, values)


def plant(drawn, rng, least, largest):
    dims = drawn.shape
    spot = [jax.random.randint(jax.random.fold_in(rng, axis), (), 0, dims[axis]) for axis in range(len(dims))]
    drawn = drawn.at[tuple(spot)].set(least)
    longest = dims.index(max(dims))
    spot[longest] = (spot[longest] + 1) % dims[longest]
    return drawn.at[tuple(spot)].set(largest)


def steps_of(key, shape, shards, smallest, high):
    level = 1.0
    for position, shards_of in shards:
        heights = jax.random.uniform(jax.random.fold_in(jax.random.fold_in(key, 6), position), (shards_of,), jnp.float32, smallest / len(shards), high / len(shards))
        level = level * jnp.repeat(jnp.exp(heights), shape[position] // shards_of).reshape((-1,) + (1,) * (len(shape) - 1 - position))
    return level


def gaussian(rng, extent, width, reach, pieces=(), kind=jnp.bfloat16):
    loudness = steps_of(rng, extent, pieces, -0.22, 0.18) if pieces else 1.0
    values = jax.random.normal(rng, extent, jnp.float32) * width * loudness
    return jnp.minimum(jnp.maximum(values, -reach), reach).astype(kind)


def setup_inputs(seed: int = 0) -> dict:
    splits = jax.random.split(jax.random.key(seed), 8)
    replica_grads = gaussian(splits[0], (REPS, D, D), 0.03, 0.19921875, ((0, 4), (1, 8)))
    weight = gaussian(splits[1], (D, D), 1.0, 6.0, ((0, 8),))
    moment_one = gaussian(splits[2], (K, K), 0.5, 3.0, ((0, 4), (1, 8)), jnp.float32)
    moment_two = jnp.clip(jnp.exp(math.log(10.0) - 4.6051702 * jax.random.uniform(splits[3], (K, K), jnp.float32) ** steps_of(splits[3], (K, K), ((0, 4), (1, 8)), -0.2, 0.2)), 0.1, 10.0)
    sign_bits = plant(jax.random.randint(splits[4], (D,), 0, 2), jax.random.fold_in(splits[4], 1), 0, 1).astype(jnp.int32)
    kept_rows = draw_kept_rows(jax.random.fold_in(splits[7], 71), 0)
    step_count = jax.random.randint(splits[6], (), 1, 8).astype(jnp.int32)
    return {"replica_grads": replica_grads, "weight": weight, "moment_one": moment_one, "moment_two": moment_two, "sign_bits": sign_bits, "kept_rows": kept_rows, "step_count": step_count}


BETA_ONE = 0.9
BETA_TWO = 0.95
EPSILON = 1e-08
LEARN_RATE = 0.25

def hadamard(order):
    positions = jnp.arange(order, dtype=jnp.int32)
    both = jnp.bitwise_and(positions[:, None], positions[None, :])
    parity = jnp.zeros_like(both)
    for bit_index in range(max(order.bit_length() - 1, 0)):
        parity = parity + jnp.bitwise_and(jnp.right_shift(both, bit_index), 1)
    parity = parity % 2
    return (1 - 2 * parity).astype(jnp.float32)

def transform_last(matrix):
    length = matrix.shape[-1]
    low_len = min(length, 128)
    high_len = length // low_len
    values = matrix.astype(jnp.float32).reshape(matrix.shape[:-1] + (high_len, low_len))
    values = jnp.einsum('rab,cb->rac', values, hadamard(low_len), precision=lax.Precision.HIGHEST)
    values = jnp.einsum('rab,ca->rcb', values, hadamard(high_len), precision=lax.Precision.HIGHEST)
    return values.reshape(matrix.shape)

def transform_rows(matrix):
    length = matrix.shape[0]
    low_len = min(length, 128)
    high_len = length // low_len
    values = matrix.astype(jnp.float32).reshape((high_len, low_len) + matrix.shape[1:])
    values = jnp.einsum('abc,db->adc', values, hadamard(low_len), precision=lax.Precision.HIGHEST)
    values = jnp.einsum('abc,da->dbc', values, hadamard(high_len), precision=lax.Precision.HIGHEST)
    return values.reshape(matrix.shape)

def reference(replica_grads, weight, moment_one, moment_two, sign_bits, kept_rows, step_count):
    sign_vec = (1 - 2 * sign_bits).astype(jnp.float32)
    norm_scale = 1.0 / math.sqrt(K)
    gsum = jnp.zeros((D, D), jnp.float32)
    for replica in range(REPS):
        gsum = gsum + replica_grads[replica].astype(jnp.float32)
    right_side = jnp.take(transform_last(gsum * sign_vec[None, :]), kept_rows, axis=1) * norm_scale
    compressed = jnp.take(transform_rows(right_side * sign_vec[:, None]), kept_rows, axis=0) * norm_scale
    new_one = BETA_ONE * moment_one + (1.0 - BETA_ONE) * compressed
    new_two = BETA_TWO * moment_two + (1.0 - BETA_TWO) * compressed * compressed
    steps_done = step_count.astype(jnp.float32)
    first_fix = 1.0 - jnp.power(jnp.float32(BETA_ONE), steps_done)
    second_fix = 1.0 - jnp.power(jnp.float32(BETA_TWO), steps_done)
    direction = new_one / first_fix / (jnp.sqrt(new_two / second_fix) + EPSILON)
    placed = jnp.zeros((D, K), jnp.float32).at[kept_rows].set(direction)
    back_bf = (transform_rows(placed) * sign_vec[:, None] * norm_scale).astype(jnp.bfloat16)
    col_fill = jnp.zeros((D, D), jnp.bfloat16).at[:, kept_rows].set(back_bf)
    update_full = transform_last(col_fill) * sign_vec[None, :] * norm_scale
    new_weight = (weight.astype(jnp.float32) - LEARN_RATE * update_full).astype(jnp.bfloat16)
    return (new_weight, new_one, new_two)
```

```python
import math

import jax
import jax.numpy as jnp
from jax import lax
from jax.sharding import PartitionSpec as P

BETA_ONE = 0.9
BETA_TWO = 0.95
EPSILON = 1e-08
LEARN_RATE = 0.25


def sketch(kept_rows, signs, start, length, scale):
    columns = start + jnp.arange(length, dtype=jnp.int32)
    both = jnp.bitwise_and(kept_rows[:, None], columns[None, :])
    odd = jnp.bitwise_and(lax.population_count(both) + signs[None, :], 1)
    return jnp.where(odd == 1, -scale, scale).astype(jnp.bfloat16)


def local(replica_grads, weight, moment_one, moment_two, sign_bits, kept_rows, step_count):
    full_len = sign_bits.shape[0]
    kept_len = kept_rows.shape[0]
    scale = 1.0 / math.sqrt(kept_len)
    rows = weight.shape[0]
    start = lax.axis_index("fsdp") * rows
    whole = sketch(kept_rows, sign_bits, 0, full_len, scale)
    mine = sketch(
        kept_rows, lax.dynamic_slice_in_dim(sign_bits, start, rows, 0), start, rows, scale
    )
    grads = replica_grads[0]
    right = lax.dot_general(
        grads, whole, (((1,), (1,)), ((), ())), preferred_element_type=jnp.float32
    ).astype(jnp.bfloat16)
    part = lax.dot_general(
        mine, right, (((1,), (0,)), ((), ())), preferred_element_type=jnp.float32
    ).astype(jnp.bfloat16)
    part = lax.psum_scatter(part, "rep", scatter_dimension=0, tiled=True)
    compressed = lax.psum_scatter(part, "fsdp", scatter_dimension=1, tiled=True).astype(
        jnp.float32
    )
    new_one = BETA_ONE * moment_one + (1.0 - BETA_ONE) * compressed
    new_two = BETA_TWO * moment_two + (1.0 - BETA_TWO) * compressed * compressed
    steps_done = step_count.astype(jnp.float32)
    first_fix = 1.0 - jnp.power(jnp.float32(BETA_ONE), steps_done)
    second_fix = 1.0 - jnp.power(jnp.float32(BETA_TWO), steps_done)
    direction = new_one / first_fix / (jnp.sqrt(new_two / second_fix) + EPSILON)
    panel = lax.all_gather(direction.astype(jnp.bfloat16), "fsdp", axis=1, tiled=True)
    panel = lax.all_gather(panel, "rep", axis=0, tiled=True)
    back = lax.dot_general(
        mine, panel, (((0,), (0,)), ((), ())), preferred_element_type=jnp.float32
    ).astype(jnp.bfloat16)
    update = lax.dot_general(
        back, whole, (((1,), (0,)), ((), ())), preferred_element_type=jnp.float32
    )
    new_weight = (weight.astype(jnp.float32) - LEARN_RATE * update).astype(jnp.bfloat16)
    return (new_weight, new_one, new_two)


def solution(mesh):
    in_specs = (
        P("rep", "fsdp", None),
        P("fsdp", None),
        P("rep", "fsdp"),
        P("rep", "fsdp"),
        P(),
        P(),
        P(),
    )
    out_specs = (P("fsdp", None), P("rep", "fsdp"), P("rep", "fsdp"))
    return jax.shard_map(local, mesh=mesh, in_specs=in_specs, out_specs=out_specs, check_vma=False)
```

```python
import functools
import math

import jax
import jax.numpy as jnp
from jax import lax
from jax.experimental import pallas as pl
from jax.experimental.pallas import tpu as pltpu
from jax.sharding import PartitionSpec as P

BETA_ONE = 0.9
BETA_TWO = 0.95
EPSILON = 1e-08
LEARN_RATE = 0.25


def sketch(kept_rows, signs, start, length, scale):
    columns = start + jnp.arange(length, dtype=jnp.int32)
    both = jnp.bitwise_and(kept_rows[:, None], columns[None, :])
    odd = jnp.bitwise_and(lax.population_count(both) + signs[None, :], 1)
    return jnp.where(odd == 1, -scale, scale).astype(jnp.bfloat16)


def adam(compressed, moment_one, moment_two, first_fix, second_fix):
    new_one = BETA_ONE * moment_one + (1.0 - BETA_ONE) * compressed
    new_two = BETA_TWO * moment_two + (1.0 - BETA_TWO) * compressed * compressed
    direction = new_one / first_fix / (jnp.sqrt(new_two / second_fix) + EPSILON)
    return new_one, new_two, direction.astype(jnp.bfloat16)


def exchange(
    wide, tall, part, one, two, fixes, panel, new_one, new_two,
    got_core, sum_core, got_x, sum_x, got_y, sum_y, got_z, gathered, send, recv,
):
    rep, fsdp = lax.axis_index("rep"), lax.axis_index("fsdp")
    x, core = rep // 2, rep % 2
    z, y = fsdp // 2, fsdp % 2
    width = one.shape[1]
    at_core = (x * 2 + (1 - core), fsdp)
    at_x = [(lax.rem(x + d, wide) * 2 + core, fsdp) for d in range(1, wide)]
    at_y = (rep, z * 2 + (1 - y))
    at_z = [(rep, lax.rem(z + d, tall) * 2 + y) for d in range(1, tall)]
    partners = [at_core, at_y] + at_x + at_z
    barrier = pltpu.get_barrier_semaphore()
    for partner in partners:
        pl.semaphore_signal(
            barrier, inc=1, device_id=partner, device_id_type=pl.DeviceIdType.MESH
        )
    pl.semaphore_wait(barrier, len(partners))

    used = [0]

    def copy(source, target, partner):
        index = used[0]
        used[0] += 1
        made = pltpu.make_async_remote_copy(
            src_ref=source,
            dst_ref=target,
            send_sem=send.at[index],
            recv_sem=recv.at[index],
            device_id=partner,
            device_id_type=pl.DeviceIdType.MESH,
        )
        made.start()
        return made

    def finish(copies):
        for made in copies:
            made.wait()

    def add(left, *others):
        total = left.astype(jnp.float32)
        for other in others:
            total = total + other.astype(jnp.float32)
        return total

    finish([copy(part.at[:, 1 - core], got_core, at_core)])
    for i in range(wide):
        sum_core[i] = add(part[i, core], got_core[i]).astype(jnp.bfloat16)
    finish(
        [
            copy(sum_core.at[lax.rem(x + d, wide)], got_x.at[d - 1], at_x[d - 1])
            for d in range(1, wide)
        ]
    )
    for i in range(2 * tall):
        columns = slice(i * width, (i + 1) * width)
        sum_x[i // 2, i % 2] = add(
            sum_core[x, :, columns], *[got_x[d, :, columns] for d in range(wide - 1)]
        ).astype(jnp.bfloat16)
    finish([copy(sum_x.at[:, 1 - y], got_y, at_y)])
    for i in range(tall):
        sum_y[i] = add(sum_x[i, y], got_y[i]).astype(jnp.bfloat16)
    finish(
        [
            copy(sum_y.at[lax.rem(z + d, tall)], got_z.at[d - 1], at_z[d - 1])
            for d in range(1, tall)
        ]
    )
    compressed = add(sum_y[z], *[got_z[d] for d in range(tall - 1)])
    new_one[...], new_two[...], gathered[z, y] = adam(
        compressed, one[...], two[...], fixes[0], fixes[1]
    )
    finish(
        [copy(gathered.at[z, y], gathered.at[z, y], at_z[d - 1]) for d in range(1, tall)]
    )
    finish([copy(gathered.at[:, y], gathered.at[:, y], at_y)])
    for i in range(2 * tall):
        panel[x, core, :, i * width : (i + 1) * width] = gathered[i // 2, i % 2]
    finish([copy(panel.at[x, core], panel.at[x, core], at_x[d - 1]) for d in range(1, wide)])
    finish([copy(panel.at[:, core], panel.at[:, core], at_core)])


def exchanged(reps, shards, part, moment_one, moment_two, fixes):
    wide, tall = reps // 2, shards // 2
    height, width = moment_one.shape
    length = part.shape[1]
    half = jnp.bfloat16
    panel, new_one, new_two = pl.pallas_call(
        functools.partial(exchange, wide, tall),
        out_shape=(
            jax.ShapeDtypeStruct((wide, 2, height, length), half),
            jax.ShapeDtypeStruct((height, width), jnp.float32),
            jax.ShapeDtypeStruct((height, width), jnp.float32),
        ),
        in_specs=[pl.BlockSpec(memory_space=pltpu.VMEM)] * 3
        + [pl.BlockSpec(memory_space=pltpu.SMEM)],
        out_specs=(pl.BlockSpec(memory_space=pltpu.VMEM),) * 3,
        scratch_shapes=[
            pltpu.VMEM((wide, height, length), half),
            pltpu.VMEM((wide, height, length), half),
            pltpu.VMEM((max(wide - 1, 1), height, length), half),
            pltpu.VMEM((tall, 2, height, width), half),
            pltpu.VMEM((tall, height, width), half),
            pltpu.VMEM((tall, height, width), half),
            pltpu.VMEM((max(tall - 1, 1), height, width), half),
            pltpu.VMEM((tall, 2, height, width), half),
            pltpu.SemaphoreType.DMA((2 * (wide + tall),)),
            pltpu.SemaphoreType.DMA((2 * (wide + tall),)),
        ],
        compiler_params=pltpu.CompilerParams(
            collective_id=0, has_side_effects=True, vmem_limit_bytes=24 * 2**20
        ),
        cost_estimate=pl.CostEstimate(
            flops=8 * height * length, bytes_accessed=6 * part.size, transcendentals=0
        ),
    )(part.reshape(wide, 2, height, length), moment_one, moment_two, fixes)
    return panel.reshape(part.shape), new_one, new_two


def local(reps, shards, replica_grads, weight, moment_one, moment_two, sign_bits, kept_rows, step_count):
    full_len = sign_bits.shape[0]
    kept_len = kept_rows.shape[0]
    scale = 1.0 / math.sqrt(kept_len)
    rows = weight.shape[0]
    start = lax.axis_index("fsdp") * rows
    whole = sketch(kept_rows, sign_bits, 0, full_len, scale)
    mine = sketch(
        kept_rows, lax.dynamic_slice_in_dim(sign_bits, start, rows, 0), start, rows, scale
    )
    grads = replica_grads[0]
    right = lax.dot_general(
        grads, whole, (((1,), (1,)), ((), ())), preferred_element_type=jnp.float32
    ).astype(jnp.bfloat16)
    part = lax.dot_general(
        mine, right, (((1,), (0,)), ((), ())), preferred_element_type=jnp.float32
    ).astype(jnp.bfloat16)
    steps_done = step_count.astype(jnp.float32)
    first_fix = 1.0 - jnp.power(jnp.float32(BETA_ONE), steps_done)
    second_fix = 1.0 - jnp.power(jnp.float32(BETA_TWO), steps_done)
    height, width = moment_one.shape
    if reps % 2 == 0 and shards % 2 == 0 and height % 16 == 0 and width % 128 == 0:
        fixes = jnp.stack([first_fix, second_fix])
        panel, new_one, new_two = exchanged(reps, shards, part, moment_one, moment_two, fixes)
    else:
        part = lax.psum_scatter(part, "rep", scatter_dimension=0, tiled=True)
        compressed = lax.psum_scatter(part, "fsdp", scatter_dimension=1, tiled=True).astype(
            jnp.float32
        )
        new_one, new_two, block = adam(
            compressed, moment_one, moment_two, first_fix, second_fix
        )
        panel = lax.all_gather(block, "fsdp", axis=1, tiled=True)
        panel = lax.all_gather(panel, "rep", axis=0, tiled=True)
    back = lax.dot_general(
        mine, panel, (((0,), (0,)), ((), ())), preferred_element_type=jnp.float32
    ).astype(jnp.bfloat16)
    update = lax.dot_general(
        back, whole, (((1,), (0,)), ((), ())), preferred_element_type=jnp.float32
    )
    new_weight = (weight.astype(jnp.float32) - LEARN_RATE * update).astype(jnp.bfloat16)
    return (new_weight, new_one, new_two)


def solution(mesh):
    in_specs = (
        P("rep", "fsdp", None),
        P("fsdp", None),
        P("rep", "fsdp"),
        P("rep", "fsdp"),
        P(),
        P(),
        P(),
    )
    out_specs = (P("fsdp", None), P("rep", "fsdp"), P("rep", "fsdp"))
    run = functools.partial(local, mesh.shape["rep"], mesh.shape["fsdp"])
    return jax.shard_map(run, mesh=mesh, in_specs=in_specs, out_specs=out_specs, check_vma=False)
```

```python
import functools
import math

import jax
import jax.numpy as jnp
from jax import lax
from jax.experimental import pallas as pl
from jax.experimental.pallas import tpu as pltpu
from jax.sharding import PartitionSpec as P

BETA_ONE = 0.9
BETA_TWO = 0.95
EPSILON = 1e-08
LEARN_RATE = 0.25


def sketch(kept_rows, signs, start, length, scale):
    columns = start + jnp.arange(length, dtype=jnp.int32)
    both = jnp.bitwise_and(kept_rows[:, None], columns[None, :])
    odd = jnp.bitwise_and(lax.population_count(both) + signs[None, :], 1)
    return jnp.where(odd == 1, -scale, scale).astype(jnp.bfloat16)


def adam(compressed, moment_one, moment_two, first_fix, second_fix):
    new_one = BETA_ONE * moment_one + (1.0 - BETA_ONE) * compressed
    new_two = BETA_TWO * moment_two + (1.0 - BETA_TWO) * compressed * compressed
    direction = new_one / first_fix / (jnp.sqrt(new_two / second_fix) + EPSILON)
    return new_one, new_two, direction.astype(jnp.bfloat16)


def exchange(
    wide, tall, part, one, two, fixes, panel, new_one, new_two,
    got_core, sum_core, got_x, sum_x, got_y, sum_y, got_z, gathered, send, recv,
):
    rep, fsdp = lax.axis_index("rep"), lax.axis_index("fsdp")
    x, core = rep // 2, rep % 2
    z, y = fsdp // 2, fsdp % 2
    width = one.shape[1]
    at_core = (x * 2 + (1 - core), fsdp)
    at_x = [(lax.rem(x + d, wide) * 2 + core, fsdp) for d in range(1, wide)]
    at_y = (rep, z * 2 + (1 - y))
    at_z = [(rep, lax.rem(z + d, tall) * 2 + y) for d in range(1, tall)]
    partners = [at_core, at_y] + at_x + at_z
    barrier = pltpu.get_barrier_semaphore()
    for partner in partners:
        pl.semaphore_signal(
            barrier, inc=1, device_id=partner, device_id_type=pl.DeviceIdType.MESH
        )
    pl.semaphore_wait(barrier, len(partners))

    used = [0]

    def copy(source, target, partner):
        index = used[0]
        used[0] += 1
        made = pltpu.make_async_remote_copy(
            src_ref=source,
            dst_ref=target,
            send_sem=send.at[index],
            recv_sem=recv.at[index],
            device_id=partner,
            device_id_type=pl.DeviceIdType.MESH,
        )
        made.start()
        return made

    def finish(copies):
        for made in copies:
            made.wait()

    def add(left, *others):
        total = left.astype(jnp.float32)
        for other in others:
            total = total + other.astype(jnp.float32)
        return total

    finish([copy(part.at[:, 1 - core], got_core, at_core)])
    for i in range(wide):
        for j in range(2 * tall):
            columns = slice(j * width, (j + 1) * width)
            sum_core[i, j % 2, j // 2] = add(
                part[i, core, :, columns], got_core[i, :, columns]
            ).astype(jnp.bfloat16)
    passed, kept = [
        [
            copy(sum_core.at[lax.rem(x + d, wide), v], got_x.at[d - 1, v], at_x[d - 1])
            for d in range(1, wide)
        ]
        for v in (1 - y, y)
    ]
    finish(passed)
    for i in range(tall):
        sum_x[1 - y, i] = add(
            sum_core[x, 1 - y, i], *[got_x[d, 1 - y, i] for d in range(wide - 1)]
        ).astype(jnp.bfloat16)
    across = copy(sum_x.at[1 - y], got_y, at_y)
    finish(kept)
    for i in range(tall):
        sum_x[y, i] = add(
            sum_core[x, y, i], *[got_x[d, y, i] for d in range(wide - 1)]
        ).astype(jnp.bfloat16)
    finish([across])
    for i in range(tall):
        sum_y[i] = add(sum_x[y, i], got_y[i]).astype(jnp.bfloat16)
    finish(
        [
            copy(sum_y.at[lax.rem(z + d, tall)], got_z.at[d - 1], at_z[d - 1])
            for d in range(1, tall)
        ]
    )
    compressed = add(sum_y[z], *[got_z[d] for d in range(tall - 1)])
    new_one[...], new_two[...], gathered[x, y, z] = adam(
        compressed, one[...], two[...], fixes[0], fixes[1]
    )
    mine = gathered.at[x, y, z]
    finish([copy(mine, mine, at_z[d - 1]) for d in range(1, tall)])
    mine, other = gathered.at[x, y], gathered.at[x, 1 - y]
    across = copy(mine, mine, at_y)
    along = [copy(mine, mine, at_x[d - 1]) for d in range(1, wide)]
    finish([across])
    along += [copy(other, other, at_x[d - 1]) for d in range(1, wide)]
    finish(along)
    for i in range(wide):
        for j in range(2 * tall):
            panel[i, core, :, j * width : (j + 1) * width] = gathered[i, j % 2, j // 2]
    finish([copy(panel.at[:, core], panel.at[:, core], at_core)])


def exchanged(reps, shards, part, moment_one, moment_two, fixes):
    wide, tall = reps // 2, shards // 2
    height, width = moment_one.shape
    length = part.shape[1]
    half = jnp.bfloat16
    panel, new_one, new_two = pl.pallas_call(
        functools.partial(exchange, wide, tall),
        out_shape=(
            jax.ShapeDtypeStruct((wide, 2, height, length), half),
            jax.ShapeDtypeStruct((height, width), jnp.float32),
            jax.ShapeDtypeStruct((height, width), jnp.float32),
        ),
        in_specs=[pl.BlockSpec(memory_space=pltpu.VMEM)] * 3
        + [pl.BlockSpec(memory_space=pltpu.SMEM)],
        out_specs=(pl.BlockSpec(memory_space=pltpu.VMEM),) * 3,
        scratch_shapes=[
            pltpu.VMEM((wide, height, length), half),
            pltpu.VMEM((wide, 2, tall, height, width), half),
            pltpu.VMEM((max(wide - 1, 1), 2, tall, height, width), half),
            pltpu.VMEM((2, tall, height, width), half),
            pltpu.VMEM((tall, height, width), half),
            pltpu.VMEM((tall, height, width), half),
            pltpu.VMEM((max(tall - 1, 1), height, width), half),
            pltpu.VMEM((wide, 2, tall, height, width), half),
            pltpu.SemaphoreType.DMA((2 * (2 * wide + tall),)),
            pltpu.SemaphoreType.DMA((2 * (2 * wide + tall),)),
        ],
        compiler_params=pltpu.CompilerParams(
            collective_id=0, has_side_effects=True, vmem_limit_bytes=24 * 2**20
        ),
        cost_estimate=pl.CostEstimate(
            flops=8 * height * length, bytes_accessed=6 * part.size, transcendentals=0
        ),
    )(part.reshape(wide, 2, height, length), moment_one, moment_two, fixes)
    return panel.reshape(part.shape), new_one, new_two


def local(reps, shards, replica_grads, weight, moment_one, moment_two, sign_bits, kept_rows, step_count):
    full_len = sign_bits.shape[0]
    kept_len = kept_rows.shape[0]
    scale = 1.0 / math.sqrt(kept_len)
    rows = weight.shape[0]
    start = lax.axis_index("fsdp") * rows
    whole = sketch(kept_rows, sign_bits, 0, full_len, scale)
    mine = sketch(
        kept_rows, lax.dynamic_slice_in_dim(sign_bits, start, rows, 0), start, rows, scale
    )
    grads = replica_grads[0]
    right = lax.dot_general(
        grads, whole, (((1,), (1,)), ((), ())), preferred_element_type=jnp.float32
    ).astype(jnp.bfloat16)
    part = lax.dot_general(
        mine, right, (((1,), (0,)), ((), ())), preferred_element_type=jnp.float32
    ).astype(jnp.bfloat16)
    steps_done = step_count.astype(jnp.float32)
    first_fix = 1.0 - jnp.power(jnp.float32(BETA_ONE), steps_done)
    second_fix = 1.0 - jnp.power(jnp.float32(BETA_TWO), steps_done)
    height, width = moment_one.shape
    if reps % 2 == 0 and shards % 2 == 0 and height % 16 == 0 and width % 128 == 0:
        fixes = jnp.stack([first_fix, second_fix])
        panel, new_one, new_two = exchanged(reps, shards, part, moment_one, moment_two, fixes)
    else:
        part = lax.psum_scatter(part, "rep", scatter_dimension=0, tiled=True)
        compressed = lax.psum_scatter(part, "fsdp", scatter_dimension=1, tiled=True).astype(
            jnp.float32
        )
        new_one, new_two, block = adam(
            compressed, moment_one, moment_two, first_fix, second_fix
        )
        panel = lax.all_gather(block, "fsdp", axis=1, tiled=True)
        panel = lax.all_gather(panel, "rep", axis=0, tiled=True)
    back = lax.dot_general(
        mine, panel, (((0,), (0,)), ((), ())), preferred_element_type=jnp.float32
    ).astype(jnp.bfloat16)
    update = lax.dot_general(
        back, whole, (((1,), (0,)), ((), ())), preferred_element_type=jnp.float32
    )
    new_weight = (weight.astype(jnp.float32) - LEARN_RATE * update).astype(jnp.bfloat16)
    return (new_weight, new_one, new_two)


def solution(mesh):
    in_specs = (
        P("rep", "fsdp", None),
        P("fsdp", None),
        P("rep", "fsdp"),
        P("rep", "fsdp"),
        P(),
        P(),
        P(),
    )
    out_specs = (P("fsdp", None), P("rep", "fsdp"), P("rep", "fsdp"))
    run = functools.partial(local, mesh.shape["rep"], mesh.shape["fsdp"])
    return jax.shard_map(run, mesh=mesh, in_specs=in_specs, out_specs=out_specs, check_vma=False)
```
